32 devices in a mesh: probe: 2 (over core), tile: 8 (over z, x), sub: 2 (over y).
Axes of the slice: x: 2, y: 2, z: 4, core: 2. Of those that a mesh axis runs over, the one named last changes fastest.
Arguments:
- base_velocity: float32 [2, 128, 256], P(None, 'tile', 'sub'), may hold values from -6 to 6
- viscosity: float32 [128, 256], P('tile', 'sub'), may hold values from 0.5 to 2
- friction: float32 [128, 256], P('tile', 'sub'), may hold values from 0.25 to 2
- cell_map: int32 [128, 256], P('tile', 'sub'), may hold values from 0 to 2047, as said below
- probe_signs: int32 [64, 2048], P('probe', ('tile', 'sub')), may hold values from 0 to 1
- param_scale: float32 [2048], P(('tile', 'sub')), may hold values from 0.5 to 2
- track_nodes: int32 [16, 16, 32, 128], P(('tile', 'sub')), may hold values from 0 to 2047
- los_coeff: float32 [2, 16, 16, 32, 128], P(None, ('tile', 'sub')), may hold values from -1 to 1
- pixel_weight: float32 [16, 16, 32, 128], P(None, ('tile', 'sub')), may hold values from 0.5 to 2
- track_precision: float32 [16, 512, 512], P(('tile', 'sub')), as said below
- slot_count: int32 [16, 16], replicated, may hold values from 0 to 32, as said below
Outputs:
- hess_probe: float32 [64, 2048], P('probe', ('tile', 'sub'))
- diag_estimate: float32 [2048], P(('tile', 'sub'))
The draws below stay inside these ranges and needn't reach their ends.
Inputs may be any that keep to these rules, and one draw needn't show every extreme that they name: `cell_map`: each node's cell belongs to the node's own mesh block: block b holds cells b * 128 to (b + 1) * 128 - 1, and each cell gathers the nodes of a small patch of its block. Slots below slot_count of a pair are live; every mesh block has some owner whose 32 slots are all live. `track_precision`: each owner's matrix is symmetric.
All inputs are finite; a program needn't handle non-finite values.
Results may differ from the reference program's by a relative error of at most 0.0013.
Values may be sent and summed in bfloat16 or wider, within the bound.
A program may use at most 128 MiB of HBM per device.

```python
import math
import jax
import jax.numpy as jnp
from jax import lax

PROBES = 64
FX = 16
FY = 128
SWEEPS = 4
PIX = 128
TILES_DEV = 512
NX = 128
NY = 256
NM = 16
SLOTS = 32
PC_DEV = 128
PCELLS = 2048
N_SUB = 2


def draw_cell_map(key, part):
    key = jax.random.fold_in(key, 11)
    key_rows, key_cols = jax.random.split(key)
    rows = jnp.arange(NX, dtype=jnp.int32)[:, None]
    cols = jnp.arange(NY, dtype=jnp.int32)[None, :]
    jitter_rows = jax.random.randint(key_rows, (NX, NY), -1, 2)
    jitter_cols = jax.random.randint(key_cols, (NX, NY), -1, 2)
    patch_row = jnp.clip(rows % FX + jitter_rows, 0, FX - 1) // 4
    patch_col = jnp.clip(cols % FY + jitter_cols, 0, FY - 1) // 4
    owner = rows // FX * (NY // FY) + cols // FY
    return (owner * PC_DEV + patch_row * (FY // 4) + patch_col).astype(jnp.int32)


def draw_slot_count(key, part):
    key = jax.random.fold_in(key, 23)
    key_base, key_shift = jax.random.split(key)
    base = jax.random.randint(key_base, (NM, NM), 0, SLOTS + 1)
    offset = jax.random.randint(key_shift, (), 0, NM)
    rows = jnp.arange(NM, dtype=jnp.int32)[:, None]
    cols = jnp.arange(NM, dtype=jnp.int32)[None, :]
    full = cols == (rows + offset) % NM
    return jnp.where(full, SLOTS, base).astype(jnp.int32)


def draw_track_precision(key, part):
    key = jax.random.fold_in(key, 37)
    spread = 0.9 / TILES_DEV ** 0.5
    raw = jax.random.uniform(key, (NM, TILES_DEV, TILES_DEV), jnp.float32, -1.0, 1.0) * spread
    sym = 0.5 * (raw + jnp.swapaxes(raw, 1, 2))
    eye = (jnp.arange(TILES_DEV)[:, None] == jnp.arange(TILES_DEV)[None, :]).astype(jnp.float32)
    return (sym + eye[None]).astype(jnp.float32)


def touch_ends(drawn, rng, low, high):
    spot = [jax.random.randint(jax.random.fold_in(rng, axis), (), 0, length) for axis, length in enumerate(drawn.shape)]
    longest = drawn.shape.index(max(drawn.shape))
    beside = spot[:longest] + [(spot[longest] + 1) % drawn.shape[longest]] + spot[longest + 1:]
    return drawn.at[tuple(spot)].set(low).at[tuple(beside)].set(high)


def level_of(rng, extent, cuts, least, largest):
    gain = 1.0
    for axis_at, parts in cuts:
        steps = jax.random.uniform(jax.random.fold_in(jax.random.fold_in(rng, 6), axis_at), (parts,), jnp.float32, least / len(cuts), largest / len(cuts))
        gain = gain * jnp.repeat(jnp.exp(steps), extent[axis_at] // parts).reshape((-1,) + (1,) * (len(extent) - 1 - axis_at))
    return gain


def normal_values(key, shape, width, most, pieces=(), held_as=jnp.bfloat16):
    factor_of = level_of(key, shape, pieces, -0.22, 0.18) if pieces else 1.0
    values = jax.random.normal(key, shape, jnp.float32) * width * factor_of
    return jnp.minimum(jnp.maximum(values, -most), most).astype(held_as)


def setup_inputs(seed: int = 0) -> dict:
    key_of = jax.random.split(jax.random.key(seed), 12)
    return {
        "base_velocity": normal_values(key_of[0], (2, NX, NY), 1.0, 6.0, ((1, 8), (2, 2)), jnp.float32),
        "viscosity": jnp.clip(jnp.exp(math.log(2.0) - 1.3862944 * jax.random.uniform(key_of[1], (NX, NY), jnp.float32) ** level_of(key_of[1], (NX, NY), ((0, 8), (1, 2)), -0.2, 0.2)), 0.5, 2.0),
        "friction": jnp.clip(jnp.exp(math.log(2.0) - 2.0794415 * jax.random.uniform(key_of[2], (NX, NY), jnp.float32) ** level_of(key_of[2], (NX, NY), ((0, 8), (1, 2)), -0.2, 0.2)), 0.25, 2.0),
        "cell_map": draw_cell_map(jax.random.fold_in(key_of[11], 71), 0),
        "probe_signs": touch_ends(jax.random.randint(key_of[4], (PROBES, PCELLS), 0, 2), jax.random.fold_in(key_of[4], 1), 0, 1).astype(jnp.int32),
        "param_scale": jnp.clip(jnp.exp(math.log(2.0) - 1.3862944 * jax.random.uniform(key_of[5], (PCELLS,), jnp.float32) ** level_of(key_of[5], (PCELLS,), ((0, 16),), -0.2, 0.2)), 0.5, 2.0),
        "track_nodes": touch_ends(jax.random.randint(key_of[6], (NM, NM, SLOTS, PIX), 0, FX * FY), jax.random.fold_in(key_of[6], 1), 0, (FX * FY) - 1).astype(jnp.int32),
        "los_coeff": jnp.clip(jax.random.uniform(key_of[7], (2, NM, NM, SLOTS, PIX), jnp.float32, -1.0, 1.0) * level_of(key_of[7], (2, NM, NM, SLOTS, PIX), ((1, 16),), -0.4, 0.0), -1.0, 1.0),
        "pixel_weight": jnp.clip(jnp.exp(math.log(2.0) - 1.3862944 * jax.random.uniform(key_of[8], (NM, NM, SLOTS, PIX), jnp.float32) ** level_of(key_of[8], (NM, NM, SLOTS, PIX), ((1, 16),), -0.2, 0.2)), 0.5, 2.0),
        "track_precision": draw_track_precision(jax.random.fold_in(key_of[11], 71), 0),
        "slot_count": draw_slot_count(jax.random.fold_in(key_of[11], 71), 0),
    }


def padded_sum(field):
    widths = [(0, 0)] * (field.ndim - 2) + [(1, 1), (1, 1)]
    padded = jnp.pad(field, widths)
    return padded[..., 2:, 1:-1] + padded[..., :-2, 1:-1] + padded[..., 1:-1, 2:] + padded[..., 1:-1, :-2]


def reference(base_velocity, viscosity, friction, cell_map, probe_signs, param_scale, track_nodes, los_coeff, pixel_weight, track_precision, slot_count):
    blocks = jnp.arange(NM, dtype=jnp.int32)[:, None, None, None]
    tile_pos = blocks // N_SUB
    sub_pos = blocks % N_SUB
    node_row = track_nodes // FY
    node_col = track_nodes % FY
    global_index = ((tile_pos * FX + node_row) * NY + sub_pos * FY + node_col).reshape(-1).astype(jnp.int32)
    slot_ids = jnp.arange(SLOTS, dtype=jnp.int32)[None, None, :, None]
    live = (slot_ids < slot_count[:, :, None, None]).astype(jnp.float32)
    weight_mask = (pixel_weight * live).reshape(-1)
    coeff = los_coeff.reshape(2, -1)
    diag_op = friction + 4.0 * viscosity
    cells = cell_map.reshape(-1)

    def one_probe(signs):
        perturb = (2 * signs - 1).astype(jnp.float32) * param_scale
        node_pert = perturb[cell_map]
        forcing_fwd = -node_pert[None] * base_velocity
        velocity = jnp.zeros_like(forcing_fwd)
        for repeat in range(SWEEPS):
            velocity = (forcing_fwd + viscosity * padded_sum(velocity)) / diag_op
        sampled = velocity.reshape(2, -1)[:, global_index]
        observed = (coeff[0] * sampled[0] + coeff[1] * sampled[1]).astype(jnp.bfloat16)
        scaled_obs = observed.astype(jnp.float32) * weight_mask
        by_owner = scaled_obs.reshape(NM, NM, SLOTS, PIX).transpose(1, 0, 2, 3).reshape(NM, TILES_DEV, PIX)
        mixed = jnp.einsum("okj,ojx->okx", track_precision, by_owner, precision=lax.Precision.HIGHEST)
        mixed = mixed.reshape(NM, NM, SLOTS, PIX).transpose(1, 0, 2, 3).reshape(-1)
        weighted = (mixed * weight_mask).astype(jnp.bfloat16)
        contrib = coeff * weighted.astype(jnp.float32)[None]
        adj_force = jnp.zeros((2, NX * NY), jnp.float32).at[:, global_index].add(contrib).reshape(2, NX, NY)
        adj_sum = jnp.zeros_like(adj_force)
        for repeat in range(SWEEPS):
            adj_sum = adj_force + padded_sum(viscosity * adj_sum / diag_op)
        adjoint_field = adj_sum / diag_op
        grad_node = -(base_velocity[0] * adjoint_field[0] + base_velocity[1] * adjoint_field[1])
        summed = jax.ops.segment_sum(grad_node.reshape(-1), cells, num_segments=PCELLS)
        return param_scale * summed

    hess_probe = lax.map(one_probe, probe_signs)
    signed = (2 * probe_signs - 1).astype(jnp.float32)
    diag_estimate = jnp.sum(signed * hess_probe, axis=0) / PROBES
    return hess_probe, diag_estimate
```

```python
import functools

import jax
import jax.numpy as jnp
from jax import lax
from jax.experimental import pallas as pl
from jax.experimental.pallas import tpu as pltpu
from jax.sharding import PartitionSpec as P

SWEEPS = 4
GROUP = 4
LANES = 128
BF = jnp.bfloat16
F32 = jnp.float32
LAST = (((1,), (1,)), ((), ()))


def owner_kernel(
    dims, counts, field, pix, weight, prec, out, base, ya, yb, track, vel, coef, pixf, phi, plo
):
    subs, rows, per, chunks, slots = dims
    blocks = field.shape[0]
    tiles = blocks // subs
    grid_rows = tiles * rows
    kp = 2 * per
    half = 256 // LANES
    groups = rows // half
    tracks = blocks * slots
    visc_at, fric_at, cell_at, scale_at = (2 * rows, 3 * rows, 4 * rows, 5 * rows)
    sign_at = scale_at + 8
    step = 4
    lane = lax.broadcasted_iota(jnp.int32, (kp, LANES), 1)

    def row(ref, *at):
        return ref[at[:-1] + (pl.ds(at[-1], 1), slice(None))]

    def wide(ref, *at, count):
        return jnp.concatenate([row(ref, *at[:-1], at[-1] + i) for i in range(count)], axis=1)

    def one_hot(index, size):
        ids = lax.broadcasted_iota(jnp.int32, (size, index.shape[1]), 0).astype(F32)
        return jnp.where(ids == index, 1.0, 0.0).astype(BF)

    pixf[...] = pix[...].astype(F32)
    high = prec[...].astype(BF)
    phi[...] = high
    plo[...] = (prec[...] - high.astype(F32)).astype(BF)
    zero_row = jnp.zeros((subs, kp, LANES), F32)
    for ref in (base, ya, yb):
        ref[0] = zero_row
        ref[grid_rows + 1] = zero_row

    @pl.loop(0, blocks)
    def _(b):
        visc = field[b, visc_at : visc_at + rows, :]
        inverse = 1.0 / (field[b, fric_at : fric_at + rows, :] + 4.0 * visc)
        coef[b, 0:rows, :] = visc * inverse
        coef[b, rows : 2 * rows, :] = inverse

    def neighbour_sum(src, at):
        centre = [src[at, s] for s in range(subs)]
        right_moved = [pltpu.roll(c, 1, 1) for c in centre]
        left_moved = [pltpu.roll(c, LANES - 1, 1) for c in centre]
        sums = []
        for s in range(subs):
            before = right_moved[s - 1] if s else 0.0
            after = left_moved[s + 1] if s + 1 < subs else 0.0
            sums.append(
                src[at - 1, s]
                + src[at + 1, s]
                + jnp.where(lane == 0, before, right_moved[s])
                + jnp.where(lane == LANES - 1, after, left_moved[s])
            )
        return sums

    def sweep(body):
        @pl.loop(0, tiles)
        def _(t):
            @pl.loop(0, rows)
            def _(r):
                body(t, r, t * rows + r + 1)

    def one_chunk(chunk):
        @pl.loop(0, blocks)
        def _(b):
            t = b // subs
            s = b % subs
            scale = row(field, b, scale_at)
            top = scale.astype(BF).astype(F32)
            mid = (scale - top).astype(BF).astype(F32)
            low = scale - top - mid
            signs = field[b, pl.ds(pl.multiple_of(sign_at + chunk * per, 8), per), :]
            left = jnp.concatenate(
                [signs, top, mid, low, jnp.zeros((5, LANES), F32)], axis=0
            ).astype(BF)
            for r0 in range(0, rows, step):
                hot = one_hot(wide(field, b, cell_at + r0, count=step), LANES)
                got = jnp.dot(left, hot, preferred_element_type=F32)
                amount = got[per : per + 1] + got[per + 1 : per + 2] + got[per + 2 : per + 3]
                for i in range(step):
                    cut = slice(i * LANES, (i + 1) * LANES)
                    pert = got[:per, cut] * amount[:, cut]
                    over = row(coef, b, rows + r0 + i)
                    for k in range(2):
                        speed = row(field, b, k * rows + r0 + i) * over
                        base[t * rows + r0 + i + 1, s, k * per : (k + 1) * per, :] = -pert * speed

        def forward(src, dst):
            def body(t, r, at):
                sums = neighbour_sum(src, at)
                for s in range(subs):
                    dst[at, s] = base[at, s] + row(coef, t * subs + s, r) * sums[s]

            sweep(body)

        src = base
        for turn in range(SWEEPS - 1):
            dst = yb if src is ya else ya
            forward(src, dst)
            src = dst
        velocity = src

        @pl.loop(0, tracks)
        def _(j):
            track[pl.ds(pl.multiple_of(j * per, 8), per), :] = jnp.zeros((per, LANES), F32)

        def masks(b, s0, n):
            return jnp.concatenate(
                [jnp.where(s0 + q < n, row(weight, b, s0 + q), 0.0) for q in range(GROUP)], axis=1
            )

        @pl.loop(0, blocks)
        def _(b):
            t = b // subs
            s = b % subs
            for g in range(groups):
                for h in range(half):
                    vel[g * kp : (g + 1) * kp, h * LANES : (h + 1) * LANES] = velocity[
                        t * rows + g * half + h + 1, s
                    ].astype(BF)
            n = counts[b]

            @pl.loop(0, (n + GROUP - 1) // GROUP)
            def _(c):
                s0 = c * GROUP
                group = wide(pixf, b, 0, s0, count=GROUP)
                hot = one_hot(wide(pixf, b, 1, s0, count=GROUP), half * LANES)
                got = jnp.dot(vel[...], hot, preferred_element_type=F32)
                picked = got[:kp]
                for g in range(1, groups):
                    picked = jnp.where(group == g, got[g * kp : (g + 1) * kp], picked)
                seen = (
                    wide(pixf, b, 2, s0, count=GROUP) * picked[:per]
                    + wide(pixf, b, 3, s0, count=GROUP) * picked[per:]
                )
                seen = seen.astype(BF).astype(F32) * masks(b, s0, n)
                for q in range(GROUP):
                    at = pl.multiple_of((b * slots + s0 + q) * per, 8)
                    track[pl.ds(at, per), :] = seen[:, q * LANES : (q + 1) * LANES]

        @pl.loop(0, per // 2)
        def _(i):
            pair = [pl.ds(2 * i + e, tracks, stride=per) for e in range(2)]
            both = jnp.concatenate([track[at, :] for at in pair], axis=1)
            top = both.astype(BF)
            low = (both - top.astype(F32)).astype(BF)
            mixed = (
                jnp.dot(phi[...], top, preferred_element_type=F32)
                + jnp.dot(plo[...], top, preferred_element_type=F32)
                + jnp.dot(phi[...], low, preferred_element_type=F32)
            )
            for e in range(2):
                track[pair[e], :] = mixed[:, e * LANES : (e + 1) * LANES]

        force = base

        @pl.loop(0, blocks)
        def _(b):
            t = b // subs
            s = b % subs
            for r in range(rows):
                force[t * rows + r + 1, s] = jnp.zeros((kp, LANES), F32)
            n = counts[b]

            @pl.loop(0, (n + GROUP - 1) // GROUP)
            def _(c):
                s0 = c * GROUP
                group = wide(pixf, b, 0, s0, count=GROUP)
                hot = one_hot(wide(pixf, b, 1, s0, count=GROUP), half * LANES)
                mixed = jnp.concatenate(
                    [
                        track[pl.ds(pl.multiple_of((b * slots + s0 + q) * per, 8), per), :]
                        for q in range(GROUP)
                    ],
                    axis=1,
                )
                back = (mixed * masks(b, s0, n)).astype(BF).astype(F32)
                both = jnp.concatenate(
                    [
                        wide(pixf, b, 2, s0, count=GROUP) * back,
                        wide(pixf, b, 3, s0, count=GROUP) * back,
                    ],
                    axis=0,
                )
                spread = jnp.concatenate(
                    [jnp.where(group == g, both, 0.0).astype(BF) for g in range(groups)], axis=0
                )
                added = lax.dot_general(spread, hot, LAST, preferred_element_type=F32)
                for g in range(groups):
                    for h in range(half):
                        force[t * rows + g * half + h + 1, s] += added[
                            g * kp : (g + 1) * kp, h * LANES : (h + 1) * LANES
                        ]

        def first(t, r, at):
            for s in range(subs):
                ya[at, s] = row(coef, t * subs + s, r) * force[at, s]

        sweep(first)

        def adjoint(src, dst):
            def body(t, r, at):
                sums = neighbour_sum(src, at)
                for s in range(subs):
                    dst[at, s] = row(coef, t * subs + s, r) * (force[at, s] + sums[s])

            sweep(body)

        src = ya
        for turn in range(SWEEPS - 2):
            dst = yb if src is ya else ya
            adjoint(src, dst)
            src = dst
        scaled = src

        @pl.loop(0, tiles)
        def _(t):
            totals = [jnp.zeros((2 * per, LANES), F32) for s in range(subs)]
            for r0 in range(0, rows, step):
                grads = [[] for s in range(subs)]
                for r in range(r0, r0 + step):
                    at = t * rows + r + 1
                    sums = neighbour_sum(scaled, at)
                    for s in range(subs):
                        b = t * subs + s
                        whole = (force[at, s] + sums[s]) * row(coef, b, rows + r)
                        grads[s].append(
                            -(
                                row(field, b, r) * whole[:per]
                                + row(field, b, rows + r) * whole[per:]
                            )
                        )
                for s in range(subs):
                    grad = jnp.concatenate(grads[s], axis=1)
                    top = grad.astype(BF)
                    low = (grad - top.astype(F32)).astype(BF)
                    hot = one_hot(wide(field, t * subs + s, cell_at + r0, count=step), LANES)
                    totals[s] += lax.dot_general(
                        jnp.concatenate([top, low], axis=0), hot, LAST, preferred_element_type=F32
                    )
            for s in range(subs):
                b = t * subs + s
                out[b, pl.ds(pl.multiple_of(chunk * per, 8), per), :] = (
                    totals[s][:per] + totals[s][per:]
                ) * row(field, b, scale_at)

    if chunks == 1:
        one_chunk(0)
    else:
        pl.loop(0, chunks)(one_chunk)


def owner_part(counts, field, pix, weight, prec, subs, rows, probes):
    blocks, planes, slots, pixels = pix.shape
    grid_rows = blocks // subs * rows
    per = probes
    while per > 8 and grid_rows * subs * 2 * per * LANES * 4 > 9 * 2**20:
        per //= 2
    grid = pltpu.VMEM((grid_rows + 2, subs, 2 * per, LANES), F32)
    vmem = pl.BlockSpec(memory_space=pltpu.VMEM)
    return pl.pallas_call(
        functools.partial(owner_kernel, (subs, rows, per, probes // per, slots)),
        out_shape=jax.ShapeDtypeStruct((blocks, probes, LANES), F32),
        in_specs=[pl.BlockSpec(memory_space=pltpu.SMEM)] + [vmem] * 4,
        out_specs=vmem,
        scratch_shapes=[
            grid,
            grid,
            grid,
            pltpu.VMEM((blocks * slots * per, LANES), F32),
            pltpu.VMEM((rows * LANES // 256 * 2 * per, 256), BF),
            pltpu.VMEM((blocks, 2 * rows, LANES), F32),
            pltpu.VMEM(pix.shape, F32),
            pltpu.VMEM(prec.shape, BF),
            pltpu.VMEM(prec.shape, BF),
        ],
        compiler_params=pltpu.CompilerParams(vmem_limit_bytes=56 * 2**20),
    )(counts, field, pix, weight, prec)


def shards(
    base_velocity,
    viscosity,
    friction,
    cell_map,
    probe_signs,
    param_scale,
    track_nodes,
    los_coeff,
    pixel_weight,
    track_precision,
    slot_count,
):
    rows, cols = viscosity.shape
    cells = param_scale.shape[0]
    probes = probe_signs.shape[0]
    subs = lax.axis_size("sub")
    both = ("tile", "sub")
    myself = lax.axis_index("tile") * subs + lax.axis_index("sub")
    signed = (2 * probe_signs - 1).astype(F32)
    mine = jnp.concatenate(
        [
            base_velocity.reshape(2 * rows, cols),
            viscosity,
            friction,
            (cell_map - myself * cells).astype(F32),
            jnp.broadcast_to(param_scale[None], (8, cells)),
            signed,
        ],
        axis=0,
    )
    field = lax.all_gather(mine, both, axis=0, tiled=False)
    nodes = track_nodes[0]
    planes = jnp.stack(
        [
            (nodes // 256).astype(BF),
            (nodes % 256).astype(BF),
            los_coeff[0, 0].astype(BF),
            los_coeff[1, 0].astype(BF),
        ],
        axis=1,
    )
    pix = lax.all_to_all(planes, both, split_axis=0, concat_axis=0, tiled=True)
    counts = jnp.take(slot_count, myself, axis=1)
    part = owner_part(
        counts, field, pix, pixel_weight[:, 0], track_precision[0], subs, rows, probes
    )
    hess_probe = lax.psum_scatter(part, both, scatter_dimension=0, tiled=False)
    total = lax.psum(jnp.sum(signed * hess_probe, axis=0), "probe")
    return (hess_probe, total / (probes * lax.axis_size("probe")))


def solution(mesh):
    placed = (
        P(None, "tile", "sub"),
        P("tile", "sub"),
        P("tile", "sub"),
        P("tile", "sub"),
        P("probe", ("tile", "sub")),
        P(("tile", "sub")),
        P(("tile", "sub"), None, None, None),
        P(None, ("tile", "sub"), None, None, None),
        P(None, ("tile", "sub"), None, None),
        P(("tile", "sub"), None, None),
        P(),
    )
    return jax.shard_map(
        shards,
        mesh=mesh,
        in_specs=placed,
        out_specs=(P("probe", ("tile", "sub")), P(("tile", "sub"))),
        check_vma=False,
    )
```

```python
import functools

import jax
import jax.numpy as jnp
from jax import lax
from jax.experimental import pallas as pl
from jax.experimental.pallas import tpu as pltpu
from jax.sharding import PartitionSpec as P

SWEEPS = 4
GROUP = 8
UNROLL = 8
LANES = 128
BF = jnp.bfloat16
F32 = jnp.float32
LAST = (((1,), (1,)), ((), ()))


def owner_kernel(
    dims, counts, field, drawn, pix, weight, prec, out, base, ya, yb, track, vel, coef, pixf, left, phi, plo
):
    subs, rows, per, chunks, slots = dims
    blocks = field.shape[0]
    tiles = blocks // subs
    grid_rows = tiles * rows
    kp = 2 * per
    half = 256 // LANES
    groups = rows // half
    tracks = blocks * slots
    visc_at, fric_at, cell_at = (2 * rows, 3 * rows, 4 * rows)
    probes = per * chunks
    step = 4
    group_size = min(GROUP, slots)
    lane = lax.broadcasted_iota(jnp.int32, (kp, LANES), 1)

    def row(ref, *at):
        return ref[at[:-1] + (pl.ds(at[-1], 1), slice(None))]

    def wide(ref, *at, count):
        return jnp.concatenate([row(ref, *at[:-1], at[-1] + i) for i in range(count)], axis=1)

    def one_hot(index, size):
        ids = lax.broadcasted_iota(jnp.int32, (size, index.shape[1]), 0).astype(F32)
        return jnp.where(ids == index, 1.0, 0.0).astype(BF)

    pixf[...] = pix[...].astype(F32)
    left[...] = drawn[...].astype(F32)
    high = prec[...].astype(BF)
    phi[...] = high
    plo[...] = (prec[...] - high.astype(F32)).astype(BF)
    zero_row = jnp.zeros((subs, kp, LANES), F32)
    for ref in (base, ya, yb):
        ref[0] = zero_row
        ref[grid_rows + 1] = zero_row

    @pl.loop(0, blocks)
    def _(b):
        visc = field[b, visc_at : visc_at + rows, :]
        inverse = 1.0 / (field[b, fric_at : fric_at + rows, :] + 4.0 * visc)
        coef[b, 0:rows, :] = visc * inverse
        coef[b, rows : 2 * rows, :] = inverse

    def neighbour_sum(src, at):
        centre = [src[at, s] for s in range(subs)]
        right_moved = [pltpu.roll(c, 1, 1) for c in centre]
        left_moved = [pltpu.roll(c, LANES - 1, 1) for c in centre]
        sums = []
        for s in range(subs):
            before = right_moved[s - 1] if s else 0.0
            after = left_moved[s + 1] if s + 1 < subs else 0.0
            sums.append(
                src[at - 1, s]
                + src[at + 1, s]
                + jnp.where(lane == 0, before, right_moved[s])
                + jnp.where(lane == LANES - 1, after, left_moved[s])
            )
        return sums

    def sweep(body):
        @pl.loop(0, tiles)
        def _(t):
            @pl.loop(0, rows // UNROLL)
            def _(c):
                for i in range(UNROLL):
                    r = c * UNROLL + i
                    body(t, r, t * rows + r + 1)

    def one_chunk(chunk):
        @pl.loop(0, blocks)
        def _(b):
            t = b // subs
            s = b % subs
            signs = left[b, pl.ds(pl.multiple_of(chunk * per, 8), per), :]
            table = jnp.concatenate([signs, left[b, probes : probes + 8, :]], axis=0).astype(BF)
            for r0 in range(0, rows, step):
                hot = one_hot(wide(field, b, cell_at + r0, count=step), LANES)
                got = jnp.dot(table, hot, preferred_element_type=F32)
                amount = got[per : per + 1] + got[per + 1 : per + 2] + got[per + 2 : per + 3]
                for i in range(step):
                    cut = slice(i * LANES, (i + 1) * LANES)
                    pert = got[:per, cut] * amount[:, cut]
                    over = row(coef, b, rows + r0 + i)
                    for k in range(2):
                        speed = row(field, b, k * rows + r0 + i) * over
                        base[t * rows + r0 + i + 1, s, k * per : (k + 1) * per, :] = -pert * speed

        def forward(src, dst):
            def body(t, r, at):
                sums = neighbour_sum(src, at)
                for s in range(subs):
                    dst[at, s] = base[at, s] + row(coef, t * subs + s, r) * sums[s]

            sweep(body)

        src = base
        for turn in range(SWEEPS - 1):
            dst = yb if src is ya else ya
            forward(src, dst)
            src = dst
        velocity = src

        @pl.loop(0, tracks)
        def _(j):
            track[pl.ds(pl.multiple_of(j * per, 8), per), :] = jnp.zeros((per, LANES), F32)

        def masks(b, s0, n):
            return jnp.concatenate(
                [jnp.where(s0 + q < n, row(weight, b, s0 + q), 0.0) for q in range(group_size)], axis=1
            )

        @pl.loop(0, blocks)
        def _(b):
            t = b // subs
            s = b % subs
            for g in range(groups):
                for h in range(half):
                    vel[g * kp : (g + 1) * kp, h * LANES : (h + 1) * LANES] = velocity[
                        t * rows + g * half + h + 1, s
                    ].astype(BF)
            n = counts[b]

            @pl.loop(0, (n + group_size - 1) // group_size)
            def _(c):
                s0 = c * group_size
                group = wide(pixf, b, s0, count=group_size)
                hot = one_hot(wide(pixf, b, slots + s0, count=group_size), half * LANES)
                got = jnp.dot(vel[...], hot, preferred_element_type=F32)
                picked = got[:kp]
                for g in range(1, groups):
                    picked = jnp.where(group == g, got[g * kp : (g + 1) * kp], picked)
                seen = (
                    wide(pixf, b, 2 * slots + s0, count=group_size) * picked[:per]
                    + wide(pixf, b, 3 * slots + s0, count=group_size) * picked[per:]
                )
                seen = seen.astype(BF).astype(F32) * masks(b, s0, n)
                for q in range(group_size):
                    at = pl.multiple_of((b * slots + s0 + q) * per, 8)
                    track[pl.ds(at, per), :] = seen[:, q * LANES : (q + 1) * LANES]

        @pl.loop(0, per // 2)
        def _(i):
            pair = [pl.ds(2 * i + e, tracks, stride=per) for e in range(2)]
            both = jnp.concatenate([track[at, :] for at in pair], axis=1)
            top = both.astype(BF)
            low = (both - top.astype(F32)).astype(BF)
            mixed = (
                jnp.dot(phi[...], top, preferred_element_type=F32)
                + jnp.dot(plo[...], top, preferred_element_type=F32)
                + jnp.dot(phi[...], low, preferred_element_type=F32)
            )
            for e in range(2):
                track[pair[e], :] = mixed[:, e * LANES : (e + 1) * LANES]

        force = base

        @pl.loop(0, blocks)
        def _(b):
            t = b // subs
            s = b % subs
            for r in range(rows):
                force[t * rows + r + 1, s] = jnp.zeros((kp, LANES), F32)
            n = counts[b]

            @pl.loop(0, (n + group_size - 1) // group_size)
            def _(c):
                s0 = c * group_size
                group = wide(pixf, b, s0, count=group_size)
                hot = one_hot(wide(pixf, b, slots + s0, count=group_size), half * LANES)
                mixed = jnp.concatenate(
                    [
                        track[pl.ds(pl.multiple_of((b * slots + s0 + q) * per, 8), per), :]
                        for q in range(group_size)
                    ],
                    axis=1,
                )
                back = (mixed * masks(b, s0, n)).astype(BF).astype(F32)
                both = jnp.concatenate(
                    [
                        wide(pixf, b, 2 * slots + s0, count=group_size) * back,
                        wide(pixf, b, 3 * slots + s0, count=group_size) * back,
                    ],
                    axis=0,
                )
                spread = jnp.concatenate(
                    [jnp.where(group == g, both, 0.0).astype(BF) for g in range(groups)], axis=0
                )
                added = lax.dot_general(spread, hot, LAST, preferred_element_type=F32)
                for g in range(groups):
                    for h in range(half):
                        force[t * rows + g * half + h + 1, s] += added[
                            g * kp : (g + 1) * kp, h * LANES : (h + 1) * LANES
                        ]

        def first(t, r, at):
            for s in range(subs):
                ya[at, s] = row(coef, t * subs + s, r) * force[at, s]

        sweep(first)

        def adjoint(src, dst):
            def body(t, r, at):
                sums = neighbour_sum(src, at)
                for s in range(subs):
                    dst[at, s] = row(coef, t * subs + s, r) * (force[at, s] + sums[s])

            sweep(body)

        src = ya
        for turn in range(SWEEPS - 2):
            dst = yb if src is ya else ya
            adjoint(src, dst)
            src = dst
        scaled = src

        @pl.loop(0, tiles)
        def _(t):
            totals = [jnp.zeros((2 * per, LANES), F32) for s in range(subs)]
            for r0 in range(0, rows, step):
                grads = [[] for s in range(subs)]
                for r in range(r0, r0 + step):
                    at = t * rows + r + 1
                    sums = neighbour_sum(scaled, at)
                    for s in range(subs):
                        b = t * subs + s
                        whole = (force[at, s] + sums[s]) * row(coef, b, rows + r)
                        grads[s].append(
                            -(
                                row(field, b, r) * whole[:per]
                                + row(field, b, rows + r) * whole[per:]
                            )
                        )
                for s in range(subs):
                    grad = jnp.concatenate(grads[s], axis=1)
                    top = grad.astype(BF)
                    low = (grad - top.astype(F32)).astype(BF)
                    hot = one_hot(wide(field, t * subs + s, cell_at + r0, count=step), LANES)
                    totals[s] += lax.dot_general(
                        jnp.concatenate([top, low], axis=0), hot, LAST, preferred_element_type=F32
                    )
            for s in range(subs):
                b = t * subs + s
                out[b, pl.ds(pl.multiple_of(chunk * per, 8), per), :] = (
                    totals[s][:per] + totals[s][per:]
                ) * (row(left, b, probes) + row(left, b, probes + 1) + row(left, b, probes + 2))

    if chunks == 1:
        one_chunk(0)
    else:
        pl.loop(0, chunks)(one_chunk)


def owner_part(counts, field, drawn, pix, weight, prec, subs, rows, probes):
    blocks, slots, pixels = weight.shape
    grid_rows = blocks // subs * rows
    per = probes
    while per > 8 and grid_rows * subs * 2 * per * LANES * 4 > 9 * 2**20:
        per //= 2
    grid = pltpu.VMEM((grid_rows + 2, subs, 2 * per, LANES), F32)
    vmem = pl.BlockSpec(memory_space=pltpu.VMEM)
    return pl.pallas_call(
        functools.partial(owner_kernel, (subs, rows, per, probes // per, slots)),
        out_shape=jax.ShapeDtypeStruct((blocks, probes, LANES), F32),
        in_specs=[pl.BlockSpec(memory_space=pltpu.SMEM)] + [vmem] * 5,
        out_specs=vmem,
        scratch_shapes=[
            grid,
            grid,
            grid,
            pltpu.VMEM((blocks * slots * per, LANES), F32),
            pltpu.VMEM((rows * LANES // 256 * 2 * per, 256), BF),
            pltpu.VMEM((blocks, 2 * rows, LANES), F32),
            pltpu.VMEM(pix.shape, F32),
            pltpu.VMEM(drawn.shape, F32),
            pltpu.VMEM(prec.shape, BF),
            pltpu.VMEM(prec.shape, BF),
        ],
        compiler_params=pltpu.CompilerParams(vmem_limit_bytes=56 * 2**20),
    )(counts, field, drawn, pix, weight, prec)


MESH = pl.DeviceIdType.MESH


def place():
    subs = lax.axis_size("sub")
    count = lax.axis_size("tile") * subs
    me = lax.axis_index("tile") * subs + lax.axis_index("sub")
    core = lax.axis_index("probe")

    def device(index):
        return {"tile": index // subs, "sub": index % subs}

    return count, me, core, device, {"probe": 1 - core}


def greet(count, me, device, partner):
    barrier = pltpu.get_barrier_semaphore()

    @pl.loop(1, count)
    def _(step):
        pl.semaphore_signal(
            barrier, inc=1, device_id=device((me + step) % count), device_id_type=MESH
        )

    pl.semaphore_signal(barrier, inc=1, device_id=partner, device_id_type=MESH)
    pl.semaphore_wait(barrier, count)


def entry_kernel(mesh_in, drawn_in, pix_in, mesh, drawn, pix, sent, came, passed, got):
    count, me, core, device, partner = place()
    greet(count, me, device, partner)

    def direct(source, peer, at):
        def copy(src, dst, k):
            return pltpu.make_async_remote_copy(
                src_ref=src,
                dst_ref=dst,
                send_sem=sent.at[k, source],
                recv_sem=came.at[k, at],
                device_id=device(peer),
                device_id_type=MESH,
            )

        return (
            copy(mesh_in.at[core], mesh.at[at, core], 0),
            copy(pix_in.at[peer, core], pix.at[at, core], 1),
            copy(drawn_in, drawn.at[at], 2),
        )

    def onward(source):
        def copy(ref, k):
            return pltpu.make_async_remote_copy(
                src_ref=ref.at[source, core],
                dst_ref=ref.at[source, core],
                send_sem=passed.at[k, source],
                recv_sem=got.at[k, source],
                device_id=partner,
                device_id_type=MESH,
            )

        return copy(mesh, 0), copy(pix, 1)

    def landed(source):
        def copy(ref, k):
            return pltpu.make_async_remote_copy(
                src_ref=ref.at[source, 1 - core],
                dst_ref=ref.at[source, 1 - core],
                send_sem=passed.at[k, source],
                recv_sem=got.at[k, source],
                device_id=partner,
                device_id_type=MESH,
            )

        return copy(mesh, 0), copy(pix, 1)

    @pl.loop(1, count)
    def _(step):
        peer = (me + step) % count
        for copy in direct(peer, peer, me):
            copy.start()

    mesh[me] = mesh_in[...]
    drawn[me] = drawn_in[...]
    pix[me] = pix_in[me]

    @pl.loop(1, count)
    def _(step):
        source = (me + count - step) % count
        first, second, third = direct(source, source, source)
        first.wait_recv()
        onward(source)[0].start()
        second.wait_recv()
        onward(source)[1].start()
        third.wait_recv()

    @pl.loop(1, count)
    def _(step):
        source = (me + count - step) % count
        for copy in landed(source):
            copy.wait_recv()
        for copy in onward(source):
            copy.wait_send()
        for copy in direct(source, source, me):
            copy.wait_send()


def entry(mesh_part, drawn, pix, count):
    vmem = pl.BlockSpec(memory_space=pltpu.VMEM)
    return pl.pallas_call(
        entry_kernel,
        out_shape=(
            jax.ShapeDtypeStruct((count,) + mesh_part.shape, mesh_part.dtype),
            jax.ShapeDtypeStruct((count,) + drawn.shape, drawn.dtype),
            jax.ShapeDtypeStruct(pix.shape, pix.dtype),
        ),
        in_specs=[vmem] * 3,
        out_specs=(vmem,) * 3,
        scratch_shapes=[
            pltpu.SemaphoreType.DMA((3, count)),
            pltpu.SemaphoreType.DMA((3, count)),
            pltpu.SemaphoreType.DMA((2, count)),
            pltpu.SemaphoreType.DMA((2, count)),
        ],
        compiler_params=pltpu.CompilerParams(
            collective_id=0, has_side_effects=True, vmem_limit_bytes=40 * 2**20
        ),
    )(mesh_part, drawn, pix)


def exit_kernel(part, signs, hess, diag, held, own, other, sent, came, side):
    count, me, core, device, partner = place()
    greet(count, me, device, partner)

    def copy(peer, at):
        return pltpu.make_async_remote_copy(
            src_ref=part.at[peer],
            dst_ref=held.at[at],
            send_sem=sent.at[peer],
            recv_sem=came.at[at],
            device_id=device(peer),
            device_id_type=MESH,
        )

    @pl.loop(1, count)
    def _(step):
        copy((me + step) % count, me).start()

    def add(step, total):
        source = (me + count - step) % count
        copy(source, source).wait_recv()
        return total + held[source]

    total = lax.fori_loop(1, count, add, part[me])
    hess[...] = total
    own[...] = jnp.broadcast_to(jnp.sum(signs[...] * total, axis=0, keepdims=True), own.shape)
    swap = pltpu.make_async_remote_copy(
        src_ref=own,
        dst_ref=other,
        send_sem=side.at[0],
        recv_sem=side.at[1],
        device_id=partner,
        device_id_type=MESH,
    )
    swap.start()

    @pl.loop(1, count)
    def _(step):
        copy((me + step) % count, me).wait_send()

    swap.wait()
    diag[...] = (own[...] + other[...]) * (1.0 / (2 * signs.shape[0]))


def exit_part(part, signs):
    count, probes, cells = part.shape
    vmem = pl.BlockSpec(memory_space=pltpu.VMEM)
    return pl.pallas_call(
        exit_kernel,
        out_shape=(
            jax.ShapeDtypeStruct((probes, cells), F32),
            jax.ShapeDtypeStruct((8, cells), F32),
        ),
        in_specs=[vmem] * 2,
        out_specs=(vmem,) * 2,
        scratch_shapes=[
            pltpu.VMEM(part.shape, F32),
            pltpu.VMEM((8, cells), F32),
            pltpu.VMEM((8, cells), F32),
            pltpu.SemaphoreType.DMA((count,)),
            pltpu.SemaphoreType.DMA((count,)),
            pltpu.SemaphoreType.DMA((2,)),
        ],
        compiler_params=pltpu.CompilerParams(
            collective_id=1, has_side_effects=True, vmem_limit_bytes=40 * 2**20
        ),
    )(part, signs)


def shards(
    base_velocity,
    viscosity,
    friction,
    cell_map,
    probe_signs,
    param_scale,
    track_nodes,
    los_coeff,
    pixel_weight,
    track_precision,
    slot_count,
):
    rows, cols = viscosity.shape
    cells = param_scale.shape[0]
    probes = probe_signs.shape[0]
    subs = lax.axis_size("sub")
    count = lax.axis_size("tile") * subs
    myself = lax.axis_index("tile") * subs + lax.axis_index("sub")
    signed = (2 * probe_signs - 1).astype(F32)
    mesh_part = jnp.concatenate(
        [
            base_velocity.reshape(2 * rows, cols),
            viscosity,
            friction,
            (cell_map - myself * cells).astype(F32),
        ],
        axis=0,
    ).reshape(2, 5 * rows // 2, cols)
    top = lax.reduce_precision(param_scale, 8, 7)
    mid = lax.reduce_precision(param_scale - top, 8, 7)
    low = param_scale - top - mid
    drawn = jnp.concatenate(
        [signed, top[None], mid[None], low[None], jnp.zeros((13, cells), F32)], axis=0
    ).astype(BF)
    nodes = track_nodes[0]
    slots = nodes.shape[1]
    planes = jnp.concatenate(
        [
            (nodes // 256).astype(BF),
            (nodes % 256).astype(BF),
            los_coeff[0, 0].astype(BF),
            los_coeff[1, 0].astype(BF),
        ],
        axis=1,
    ).reshape(count, 2, 2 * slots, LANES)
    field, drawn, pix = entry(mesh_part, drawn, planes, count)
    counts = jnp.take(slot_count, myself, axis=1)
    part = owner_part(
        counts,
        field.reshape(count, 5 * rows, cols),
        drawn,
        pix.reshape(count, 4 * slots, LANES),
        pixel_weight[:, 0],
        track_precision[0],
        subs,
        rows,
        probes,
    )
    hess_probe, diag = exit_part(part, signed)
    return (hess_probe, diag[0])


def solution(mesh):
    placed = (
        P(None, "tile", "sub"),
        P("tile", "sub"),
        P("tile", "sub"),
        P("tile", "sub"),
        P("probe", ("tile", "sub")),
        P(("tile", "sub")),
        P(("tile", "sub"), None, None, None),
        P(None, ("tile", "sub"), None, None, None),
        P(None, ("tile", "sub"), None, None),
        P(("tile", "sub"), None, None),
        P(),
    )
    return jax.shard_map(
        shards,
        mesh=mesh,
        in_specs=placed,
        out_specs=(P("probe", ("tile", "sub")), P(("tile", "sub"))),
        check_vma=False,
    )
```

```python
import functools

import jax
import jax.numpy as jnp
from jax import lax
from jax.experimental import pallas as pl
from jax.experimental.pallas import tpu as pltpu
from jax.sharding import PartitionSpec as P

SWEEPS = 4
GROUP = 8
PAD = 8
UNROLL = 16
LANES = 128
BF = jnp.bfloat16
F32 = jnp.float32
LAST = (((1,), (1,)), ((), ()))


def owner_kernel(
    dims, counts, field, drawn, pix, weight_in, prec_in, out, base, ya, yb, track, vel, coef, pixf, left, phi, plo, weight, prec, fetched
):
    subs, rows, per, chunks, slots = dims
    blocks = field.shape[0]
    tiles = blocks // subs
    grid_rows = tiles * rows
    kp = 2 * per
    half = 256 // LANES
    groups = rows // half
    tracks = blocks * slots
    visc_at, fric_at, cell_at = (2 * rows, 3 * rows, 4 * rows)
    probes = per * chunks
    step = 4
    group_size = min(GROUP, slots)
    unroll = min(UNROLL, rows)
    pitch = per + PAD
    lane = lax.broadcasted_iota(jnp.int32, (kp, LANES), 1)

    def row(ref, *at):
        return ref[at[:-1] + (pl.ds(at[-1], 1), slice(None))]

    def wide(ref, *at, count):
        return jnp.concatenate([row(ref, *at[:-1], at[-1] + i) for i in range(count)], axis=1)

    def one_hot(index, size):
        ids = lax.broadcasted_iota(jnp.int32, (size, index.shape[1]), 0).astype(F32)
        return jnp.where(ids == index, 1.0, 0.0).astype(BF)

    pixf[...] = pix[...].astype(F32)
    left[...] = drawn[...].astype(F32)
    fetches = (
        pltpu.make_async_copy(weight_in, weight, fetched.at[0]),
        pltpu.make_async_copy(prec_in, prec, fetched.at[1]),
    )
    for fetch in fetches:
        fetch.start()

    def finish_fetches():
        for fetch in fetches:
            fetch.wait()
        high = prec[...].astype(BF)
        phi[...] = high
        plo[...] = (prec[...] - high.astype(F32)).astype(BF)

    zero_row = jnp.zeros((subs, kp, LANES), F32)
    for ref in (base, ya, yb):
        ref[0] = zero_row
        ref[grid_rows + 1] = zero_row

    @pl.loop(0, blocks)
    def _(b):
        visc = field[b, visc_at : visc_at + rows, :]
        inverse = 1.0 / (field[b, fric_at : fric_at + rows, :] + 4.0 * visc)
        coef[b, 0:rows, :] = visc * inverse
        coef[b, rows : 2 * rows, :] = inverse

    def neighbour_sum(src, at):
        centre = [src[at, s] for s in range(subs)]
        right_moved = [pltpu.roll(c, 1, 1) for c in centre]
        left_moved = [pltpu.roll(c, LANES - 1, 1) for c in centre]
        sums = []
        for s in range(subs):
            before = right_moved[s - 1] if s else 0.0
            after = left_moved[s + 1] if s + 1 < subs else 0.0
            sums.append(
                src[at - 1, s]
                + src[at + 1, s]
                + jnp.where(lane == 0, before, right_moved[s])
                + jnp.where(lane == LANES - 1, after, left_moved[s])
            )
        return sums

    def sweep(body):
        @pl.loop(0, tiles)
        def _(t):
            @pl.loop(0, rows // unroll)
            def _(c):
                for i in range(unroll):
                    r = c * unroll + i
                    body(t, r, t * rows + r + 1)

    def one_chunk(chunk):
        @pl.loop(0, blocks)
        def _(b):
            t = b // subs
            s = b % subs
            signs = left[b, pl.ds(pl.multiple_of(chunk * per, 8), per), :]
            table = jnp.concatenate([signs, left[b, probes : probes + 8, :]], axis=0).astype(BF)
            for r0 in range(0, rows, step):
                hot = one_hot(wide(field, b, cell_at + r0, count=step), LANES)
                got = jnp.dot(table, hot, preferred_element_type=F32)
                amount = got[per : per + 1] + got[per + 1 : per + 2] + got[per + 2 : per + 3]
                for i in range(step):
                    cut = slice(i * LANES, (i + 1) * LANES)
                    pert = got[:per, cut] * amount[:, cut]
                    over = row(coef, b, rows + r0 + i)
                    for k in range(2):
                        speed = row(field, b, k * rows + r0 + i) * over
                        base[t * rows + r0 + i + 1, s, k * per : (k + 1) * per, :] = -pert * speed

        def forward(src, dst):
            def body(t, r, at):
                sums = neighbour_sum(src, at)
                for s in range(subs):
                    dst[at, s] = base[at, s] + row(coef, t * subs + s, r) * sums[s]

            sweep(body)

        src = base
        for turn in range(SWEEPS - 1):
            dst = yb if src is ya else ya
            forward(src, dst)
            src = dst
        velocity = src
        if chunks == 1:
            finish_fetches()

        def masks(b, s0, n):
            return jnp.concatenate(
                [jnp.where(s0 + q < n, row(weight, b, s0 + q), 0.0) for q in range(group_size)], axis=1
            )

        @pl.loop(0, blocks)
        def _(b):
            t = b // subs
            s = b % subs
            for g in range(groups):
                for h in range(half):
                    vel[g * kp : (g + 1) * kp, h * LANES : (h + 1) * LANES] = velocity[
                        t * rows + g * half + h + 1, s
                    ].astype(BF)
            n = counts[b]

            @pl.loop(0, (n + group_size - 1) // group_size)
            def _(c):
                s0 = c * group_size
                group = wide(pixf, b, s0, count=group_size)
                hot = one_hot(wide(pixf, b, slots + s0, count=group_size), half * LANES)
                got = jnp.dot(vel[...], hot, preferred_element_type=F32)
                picked = got[:kp]
                for g in range(1, groups):
                    picked = jnp.where(group == g, got[g * kp : (g + 1) * kp], picked)
                seen = (
                    wide(pixf, b, 2 * slots + s0, count=group_size) * picked[:per]
                    + wide(pixf, b, 3 * slots + s0, count=group_size) * picked[per:]
                )
                seen = seen.astype(BF).astype(F32) * masks(b, s0, n)
                for q in range(group_size):
                    at = pl.multiple_of((b * slots + s0 + q) * pitch, 8)
                    track[pl.ds(at, per), :] = seen[:, q * LANES : (q + 1) * LANES]

            @pl.loop((n + group_size - 1) // group_size, slots // group_size)
            def _(c):
                for q in range(group_size):
                    at = pl.multiple_of((b * slots + c * group_size + q) * pitch, 8)
                    track[pl.ds(at, per), :] = jnp.zeros((per, LANES), F32)

        @pl.loop(0, per // 2, unroll=2)
        def _(i):
            pair = [pl.ds(2 * i + e, tracks, stride=pitch) for e in range(2)]
            both = jnp.concatenate([track[at, :] for at in pair], axis=1)
            top = both.astype(BF)
            mixed = (
                jnp.dot(phi[...], top, preferred_element_type=F32)
                + jnp.dot(plo[...], top, preferred_element_type=F32)
            )
            for e in range(2):
                track[pair[e], :] = mixed[:, e * LANES : (e + 1) * LANES]

        force = base

        @pl.loop(0, blocks)
        def _(b):
            t = b // subs
            s = b % subs
            for r in range(rows):
                force[t * rows + r + 1, s] = jnp.zeros((kp, LANES), F32)
            n = counts[b]

            @pl.loop(0, (n + group_size - 1) // group_size)
            def _(c):
                s0 = c * group_size
                group = wide(pixf, b, s0, count=group_size)
                hot = one_hot(wide(pixf, b, slots + s0, count=group_size), half * LANES)
                mixed = jnp.concatenate(
                    [
                        track[pl.ds(pl.multiple_of((b * slots + s0 + q) * pitch, 8), per), :]
                        for q in range(group_size)
                    ],
                    axis=1,
                )
                back = (mixed * masks(b, s0, n)).astype(BF).astype(F32)
                both = jnp.concatenate(
                    [
                        wide(pixf, b, 2 * slots + s0, count=group_size) * back,
                        wide(pixf, b, 3 * slots + s0, count=group_size) * back,
                    ],
                    axis=0,
                )
                spread = jnp.concatenate(
                    [jnp.where(group == g, both, 0.0).astype(BF) for g in range(groups)], axis=0
                )
                added = lax.dot_general(spread, hot, LAST, preferred_element_type=F32)
                for g in range(groups):
                    for h in range(half):
                        force[t * rows + g * half + h + 1, s] += added[
                            g * kp : (g + 1) * kp, h * LANES : (h + 1) * LANES
                        ]

        def first(t, r, at):
            for s in range(subs):
                ya[at, s] = row(coef, t * subs + s, r) * force[at, s]

        sweep(first)

        def adjoint(src, dst):
            def body(t, r, at):
                sums = neighbour_sum(src, at)
                for s in range(subs):
                    dst[at, s] = row(coef, t * subs + s, r) * (force[at, s] + sums[s])

            sweep(body)

        src = ya
        for turn in range(SWEEPS - 2):
            dst = yb if src is ya else ya
            adjoint(src, dst)
            src = dst
        scaled = src

        @pl.loop(0, tiles)
        def _(t):
            totals = [jnp.zeros((2 * per, LANES), F32) for s in range(subs)]
            for r0 in range(0, rows, step):
                grads = [[] for s in range(subs)]
                for r in range(r0, r0 + step):
                    at = t * rows + r + 1
                    sums = neighbour_sum(scaled, at)
                    for s in range(subs):
                        b = t * subs + s
                        whole = (force[at, s] + sums[s]) * row(coef, b, rows + r)
                        grads[s].append(
                            -(
                                row(field, b, r) * whole[:per]
                                + row(field, b, rows + r) * whole[per:]
                            )
                        )
                for s in range(subs):
                    grad = jnp.concatenate(grads[s], axis=1)
                    top = grad.astype(BF)
                    low = (grad - top.astype(F32)).astype(BF)
                    hot = one_hot(wide(field, t * subs + s, cell_at + r0, count=step), LANES)
                    totals[s] += lax.dot_general(
                        jnp.concatenate([top, low], axis=0), hot, LAST, preferred_element_type=F32
                    )
            for s in range(subs):
                b = t * subs + s
                out[b, pl.ds(pl.multiple_of(chunk * per, 8), per), :] = (
                    totals[s][:per] + totals[s][per:]
                ) * (row(left, b, probes) + row(left, b, probes + 1) + row(left, b, probes + 2))

    if chunks == 1:
        one_chunk(0)
    else:
        finish_fetches()
        pl.loop(0, chunks)(one_chunk)


def owner_part(counts, field, drawn, pix, weight, prec, subs, rows, probes):
    blocks, slots, pixels = weight.shape
    grid_rows = blocks // subs * rows
    per = probes
    while per > 8 and grid_rows * subs * 2 * per * LANES * 4 > 9 * 2**20:
        per //= 2
    grid = pltpu.VMEM((grid_rows + 2, subs, 2 * per, LANES), F32)
    vmem = pl.BlockSpec(memory_space=pltpu.VMEM)
    return pl.pallas_call(
        functools.partial(owner_kernel, (subs, rows, per, probes // per, slots)),
        out_shape=jax.ShapeDtypeStruct((blocks, probes, LANES), F32),
        in_specs=[pl.BlockSpec(memory_space=pltpu.SMEM)] + [vmem] * 3 + [pl.BlockSpec(memory_space=pl.ANY)] * 2,
        out_specs=vmem,
        scratch_shapes=[
            grid,
            grid,
            grid,
            pltpu.VMEM((blocks * slots * (per + PAD), LANES), F32),
            pltpu.VMEM((rows * LANES // 256 * 2 * per, 256), BF),
            pltpu.VMEM((blocks, 2 * rows, LANES), F32),
            pltpu.VMEM(pix.shape, F32),
            pltpu.VMEM(drawn.shape, F32),
            pltpu.VMEM(prec.shape, BF),
            pltpu.VMEM(prec.shape, BF),
            pltpu.VMEM(weight.shape, F32),
            pltpu.VMEM(prec.shape, F32),
            pltpu.SemaphoreType.DMA((2,)),
        ],
        compiler_params=pltpu.CompilerParams(vmem_limit_bytes=56 * 2**20),
    )(counts, field, drawn, pix, weight, prec)


MESH = pl.DeviceIdType.MESH


def place():
    subs = lax.axis_size("sub")
    count = lax.axis_size("tile") * subs
    me = lax.axis_index("tile") * subs + lax.axis_index("sub")
    core = lax.axis_index("probe")

    def device(index):
        return {"tile": index // subs, "sub": index % subs}

    return count, me, core, device, {"probe": 1 - core}


def greet(count, me, device, partner):
    barrier = pltpu.get_barrier_semaphore()

    @pl.loop(1, count)
    def _(step):
        pl.semaphore_signal(
            barrier, inc=1, device_id=device((me + step) % count), device_id_type=MESH
        )

    pl.semaphore_signal(barrier, inc=1, device_id=partner, device_id_type=MESH)
    pl.semaphore_wait(barrier, count)


def entry_kernel(mesh_in, drawn_in, pix_in, mesh, drawn, pix, sent, came, passed, got):
    count, me, core, device, partner = place()
    greet(count, me, device, partner)

    def direct(source, peer, at):
        def copy(src, dst, k):
            return pltpu.make_async_remote_copy(
                src_ref=src,
                dst_ref=dst,
                send_sem=sent.at[k, source],
                recv_sem=came.at[k, at],
                device_id=device(peer),
                device_id_type=MESH,
            )

        return (
            copy(mesh_in.at[core], mesh.at[at, core], 0),
            copy(pix_in.at[peer, core], pix.at[at, core], 1),
            copy(drawn_in, drawn.at[at], 2),
        )

    def onward(source):
        def copy(ref, k):
            return pltpu.make_async_remote_copy(
                src_ref=ref.at[source, core],
                dst_ref=ref.at[source, core],
                send_sem=passed.at[k, source],
                recv_sem=got.at[k, source],
                device_id=partner,
                device_id_type=MESH,
            )

        return copy(mesh, 0), copy(pix, 1)

    def landed(source):
        def copy(ref, k):
            return pltpu.make_async_remote_copy(
                src_ref=ref.at[source, 1 - core],
                dst_ref=ref.at[source, 1 - core],
                send_sem=passed.at[k, source],
                recv_sem=got.at[k, source],
                device_id=partner,
                device_id_type=MESH,
            )

        return copy(mesh, 0), copy(pix, 1)

    @pl.loop(1, count)
    def _(step):
        peer = (me + step) % count
        for copy in direct(peer, peer, me):
            copy.start()

    mesh[me] = mesh_in[...]
    drawn[me] = drawn_in[...]
    pix[me] = pix_in[me]

    @pl.loop(1, count)
    def _(step):
        source = (me + count - step) % count
        first, second, third = direct(source, source, source)
        first.wait_recv()
        onward(source)[0].start()
        second.wait_recv()
        onward(source)[1].start()
        third.wait_recv()

    @pl.loop(1, count)
    def _(step):
        source = (me + count - step) % count
        for copy in landed(source):
            copy.wait_recv()
        for copy in onward(source):
            copy.wait_send()
        for copy in direct(source, source, me):
            copy.wait_send()


def entry(mesh_part, drawn, pix, count):
    vmem = pl.BlockSpec(memory_space=pltpu.VMEM)
    return pl.pallas_call(
        entry_kernel,
        out_shape=(
            jax.ShapeDtypeStruct((count,) + mesh_part.shape, mesh_part.dtype),
            jax.ShapeDtypeStruct((count,) + drawn.shape, drawn.dtype),
            jax.ShapeDtypeStruct(pix.shape, pix.dtype),
        ),
        in_specs=[vmem] * 3,
        out_specs=(vmem,) * 3,
        scratch_shapes=[
            pltpu.SemaphoreType.DMA((3, count)),
            pltpu.SemaphoreType.DMA((3, count)),
            pltpu.SemaphoreType.DMA((2, count)),
            pltpu.SemaphoreType.DMA((2, count)),
        ],
        compiler_params=pltpu.CompilerParams(
            collective_id=0, has_side_effects=True, vmem_limit_bytes=40 * 2**20
        ),
    )(mesh_part, drawn, pix)


def exit_kernel(part, signs, hess, diag, held, own, other, sent, came, side):
    count, me, core, device, partner = place()
    greet(count, me, device, partner)

    def copy(peer, at):
        return pltpu.make_async_remote_copy(
            src_ref=part.at[peer],
            dst_ref=held.at[at],
            send_sem=sent.at[peer],
            recv_sem=came.at[at],
            device_id=device(peer),
            device_id_type=MESH,
        )

    @pl.loop(1, count)
    def _(step):
        copy((me + step) % count, me).start()

    def add(step, total):
        source = (me + count - step) % count
        copy(source, source).wait_recv()
        return total + held[source]

    total = lax.fori_loop(1, count, add, part[me])
    hess[...] = total
    own[...] = jnp.broadcast_to(jnp.sum(signs[...] * total, axis=0, keepdims=True), own.shape)
    swap = pltpu.make_async_remote_copy(
        src_ref=own,
        dst_ref=other,
        send_sem=side.at[0],
        recv_sem=side.at[1],
        device_id=partner,
        device_id_type=MESH,
    )
    swap.start()

    @pl.loop(1, count)
    def _(step):
        copy((me + step) % count, me).wait_send()

    swap.wait()
    diag[...] = (own[...] + other[...]) * (1.0 / (2 * signs.shape[0]))


def exit_part(part, signs):
    count, probes, cells = part.shape
    vmem = pl.BlockSpec(memory_space=pltpu.VMEM)
    return pl.pallas_call(
        exit_kernel,
        out_shape=(
            jax.ShapeDtypeStruct((probes, cells), F32),
            jax.ShapeDtypeStruct((8, cells), F32),
        ),
        in_specs=[vmem] * 2,
        out_specs=(vmem,) * 2,
        scratch_shapes=[
            pltpu.VMEM(part.shape, F32),
            pltpu.VMEM((8, cells), F32),
            pltpu.VMEM((8, cells), F32),
            pltpu.SemaphoreType.DMA((count,)),
            pltpu.SemaphoreType.DMA((count,)),
            pltpu.SemaphoreType.DMA((2,)),
        ],
        compiler_params=pltpu.CompilerParams(
            collective_id=1, has_side_effects=True, vmem_limit_bytes=40 * 2**20
        ),
    )(part, signs)


def shards(
    base_velocity,
    viscosity,
    friction,
    cell_map,
    probe_signs,
    param_scale,
    track_nodes,
    los_coeff,
    pixel_weight,
    track_precision,
    slot_count,
):
    rows, cols = viscosity.shape
    cells = param_scale.shape[0]
    probes = probe_signs.shape[0]
    subs = lax.axis_size("sub")
    count = lax.axis_size("tile") * subs
    myself = lax.axis_index("tile") * subs + lax.axis_index("sub")
    signed = (2 * probe_signs - 1).astype(F32)
    mesh_part = jnp.concatenate(
        [
            base_velocity.reshape(2 * rows, cols),
            viscosity,
            friction,
            (cell_map - myself * cells).astype(F32),
        ],
        axis=0,
    ).reshape(2, 5 * rows // 2, cols)
    top = lax.reduce_precision(param_scale, 8, 7)
    mid = lax.reduce_precision(param_scale - top, 8, 7)
    low = param_scale - top - mid
    drawn = jnp.concatenate(
        [signed, top[None], mid[None], low[None], jnp.zeros((13, cells), F32)], axis=0
    ).astype(BF)
    nodes = track_nodes[0]
    slots = nodes.shape[1]
    planes = jnp.concatenate(
        [
            (nodes // 256).astype(BF),
            (nodes % 256).astype(BF),
            los_coeff[0, 0].astype(BF),
            los_coeff[1, 0].astype(BF),
        ],
        axis=1,
    ).reshape(count, 2, 2 * slots, LANES)
    field, drawn, pix = entry(mesh_part, drawn, planes, count)
    counts = jnp.take(slot_count, myself, axis=1)
    part = owner_part(
        counts,
        field.reshape(count, 5 * rows, cols),
        drawn,
        pix.reshape(count, 4 * slots, LANES),
        pixel_weight[:, 0],
        track_precision[0],
        subs,
        rows,
        probes,
    )
    hess_probe, diag = exit_part(part, signed)
    return (hess_probe, diag[0])


def solution(mesh):
    placed = (
        P(None, "tile", "sub"),
        P("tile", "sub"),
        P("tile", "sub"),
        P("tile", "sub"),
        P("probe", ("tile", "sub")),
        P(("tile", "sub")),
        P(("tile", "sub"), None, None, None),
        P(None, ("tile", "sub"), None, None, None),
        P(None, ("tile", "sub"), None, None),
        P(("tile", "sub"), None, None),
        P(),
    )
    return jax.shard_map(
        shards,
        mesh=mesh,
        in_specs=placed,
        out_specs=(P("probe", ("tile", "sub")), P(("tile", "sub"))),
        check_vma=False,
    )
```

```python
import functools

import jax
import jax.numpy as jnp
from jax import lax
from jax.experimental import pallas as pl
from jax.experimental.pallas import tpu as pltpu
from jax.sharding import PartitionSpec as P

SWEEPS = 4
GROUP = 16
PAD = 8
UNROLL = 16
LANES = 128
BF = jnp.bfloat16
F32 = jnp.float32
LAST = (((1,), (1,)), ((), ()))


def owner_kernel(
    dims, counts, field, drawn, pix, weight_in, prec_in, out, base, ya, yb, track, vel, coef, pixf, left, phi, plo, weight, prec, fetched
):
    subs, rows, per, chunks, slots = dims
    blocks = field.shape[0]
    tiles = blocks // subs
    grid_rows = tiles * rows
    kp = 2 * per
    half = 256 // LANES
    groups = rows // half
    tracks = blocks * slots
    visc_at, fric_at, cell_at = (2 * rows, 3 * rows, 4 * rows)
    probes = per * chunks
    step = 4
    group_size = min(GROUP, slots)
    unroll = min(UNROLL, rows)
    pitch = per + PAD
    lane = lax.broadcasted_iota(jnp.int32, (kp, LANES), 1)

    def row(ref, *at):
        return ref[at[:-1] + (pl.ds(at[-1], 1), slice(None))]

    def wide(ref, *at, count):
        return jnp.concatenate([row(ref, *at[:-1], at[-1] + i) for i in range(count)], axis=1)

    def one_hot(index, size):
        ids = lax.broadcasted_iota(jnp.int32, (size, index.shape[1]), 0).astype(F32)
        return jnp.where(ids == index, 1.0, 0.0).astype(BF)

    pixf[...] = pix[...].astype(F32)
    left[...] = drawn[...].astype(F32)
    fetches = (
        pltpu.make_async_copy(weight_in, weight, fetched.at[0]),
        pltpu.make_async_copy(prec_in, prec, fetched.at[1]),
    )
    for fetch in fetches:
        fetch.start()

    def finish_fetches():
        for fetch in fetches:
            fetch.wait()
        high = prec[...].astype(BF)
        phi[...] = high
        plo[...] = (prec[...] - high.astype(F32)).astype(BF)

    zero_row = jnp.zeros((subs, kp, LANES), F32)
    for ref in (base, ya, yb):
        ref[0] = zero_row
        ref[grid_rows + 1] = zero_row

    @pl.loop(0, blocks)
    def _(b):
        visc = field[b, visc_at : visc_at + rows, :]
        inverse = 1.0 / (field[b, fric_at : fric_at + rows, :] + 4.0 * visc)
        coef[b, 0:rows, :] = visc * inverse
        coef[b, rows : 2 * rows, :] = inverse

    def neighbour_sum(src, at):
        centre = [src[at, s] for s in range(subs)]
        right_moved = [pltpu.roll(c, 1, 1) for c in centre]
        left_moved = [pltpu.roll(c, LANES - 1, 1) for c in centre]
        sums = []
        for s in range(subs):
            before = right_moved[s - 1] if s else 0.0
            after = left_moved[s + 1] if s + 1 < subs else 0.0
            sums.append(
                src[at - 1, s]
                + src[at + 1, s]
                + jnp.where(lane == 0, before, right_moved[s])
                + jnp.where(lane == LANES - 1, after, left_moved[s])
            )
        return sums

    def sweep(body):
        @pl.loop(0, tiles)
        def _(t):
            @pl.loop(0, rows // unroll)
            def _(c):
                for i in range(unroll):
                    r = c * unroll + i
                    body(t, r, t * rows + r + 1)

    def one_chunk(chunk):
        @pl.loop(0, blocks)
        def _(b):
            t = b // subs
            s = b % subs
            signs = left[b, pl.ds(pl.multiple_of(chunk * per, 8), per), :]
            table = jnp.concatenate([signs, left[b, probes : probes + 8, :]], axis=0).astype(BF)
            for r0 in range(0, rows, step):
                hot = one_hot(wide(field, b, cell_at + r0, count=step), LANES)
                got = jnp.dot(table, hot, preferred_element_type=F32)
                amount = got[per : per + 1] + got[per + 1 : per + 2] + got[per + 2 : per + 3]
                for i in range(step):
                    cut = slice(i * LANES, (i + 1) * LANES)
                    pert = got[:per, cut] * amount[:, cut]
                    over = row(coef, b, rows + r0 + i)
                    for k in range(2):
                        speed = row(field, b, k * rows + r0 + i) * over
                        base[t * rows + r0 + i + 1, s, k * per : (k + 1) * per, :] = -pert * speed

        def forward(src, dst):
            def body(t, r, at):
                sums = neighbour_sum(src, at)
                for s in range(subs):
                    dst[at, s] = base[at, s] + row(coef, t * subs + s, r) * sums[s]

            sweep(body)

        src = base
        for turn in range(SWEEPS - 1):
            dst = yb if src is ya else ya
            forward(src, dst)
            src = dst
        velocity = src
        if chunks == 1:
            finish_fetches()

        def masks(b, s0, n):
            return jnp.concatenate(
                [jnp.where(s0 + q < n, row(weight, b, s0 + q), 0.0) for q in range(group_size)], axis=1
            )

        @pl.loop(0, blocks)
        def _(b):
            t = b // subs
            s = b % subs
            for g in range(groups):
                for h in range(half):
                    vel[g * kp : (g + 1) * kp, h * LANES : (h + 1) * LANES] = velocity[
                        t * rows + g * half + h + 1, s
                    ].astype(BF)
            n = counts[b]

            @pl.loop(0, (n + group_size - 1) // group_size)
            def _(c):
                s0 = c * group_size
                group = wide(pixf, b, s0, count=group_size)
                hot = one_hot(wide(pixf, b, slots + s0, count=group_size), half * LANES)
                got = jnp.dot(vel[...], hot, preferred_element_type=F32)
                picked = got[:kp]
                for g in range(1, groups):
                    picked = jnp.where(group == g, got[g * kp : (g + 1) * kp], picked)
                seen = (
                    wide(pixf, b, 2 * slots + s0, count=group_size) * picked[:per]
                    + wide(pixf, b, 3 * slots + s0, count=group_size) * picked[per:]
                )
                seen = seen.astype(BF).astype(F32) * masks(b, s0, n)
                for q in range(group_size):
                    at = pl.multiple_of((b * slots + s0 + q) * pitch, 8)
                    track[pl.ds(at, per), :] = seen[:, q * LANES : (q + 1) * LANES]

            @pl.loop((n + group_size - 1) // group_size, slots // group_size)
            def _(c):
                for q in range(group_size):
                    at = pl.multiple_of((b * slots + c * group_size + q) * pitch, 8)
                    track[pl.ds(at, per), :] = jnp.zeros((per, LANES), F32)

        @pl.loop(0, per // 2, unroll=4)
        def _(i):
            pair = [pl.ds(2 * i + e, tracks, stride=pitch) for e in range(2)]
            both = jnp.concatenate([track[at, :] for at in pair], axis=1)
            top = both.astype(BF)
            mixed = (
                jnp.dot(phi[...], top, preferred_element_type=F32)
                + jnp.dot(plo[...], top, preferred_element_type=F32)
            )
            for e in range(2):
                track[pair[e], :] = mixed[:, e * LANES : (e + 1) * LANES]

        force = base

        @pl.loop(0, blocks)
        def _(b):
            t = b // subs
            s = b % subs
            for r in range(rows):
                force[t * rows + r + 1, s] = jnp.zeros((kp, LANES), F32)
            n = counts[b]

            @pl.loop(0, (n + group_size - 1) // group_size)
            def _(c):
                s0 = c * group_size
                group = wide(pixf, b, s0, count=group_size)
                hot = one_hot(wide(pixf, b, slots + s0, count=group_size), half * LANES)
                mixed = jnp.concatenate(
                    [
                        track[pl.ds(pl.multiple_of((b * slots + s0 + q) * pitch, 8), per), :]
                        for q in range(group_size)
                    ],
                    axis=1,
                )
                back = (mixed * masks(b, s0, n)).astype(BF).astype(F32)
                both = jnp.concatenate(
                    [
                        wide(pixf, b, 2 * slots + s0, count=group_size) * back,
                        wide(pixf, b, 3 * slots + s0, count=group_size) * back,
                    ],
                    axis=0,
                )
                spread = jnp.concatenate(
                    [jnp.where(group == g, both, 0.0).astype(BF) for g in range(groups)], axis=0
                )
                added = lax.dot_general(spread, hot, LAST, preferred_element_type=F32)
                for g in range(groups):
                    for h in range(half):
                        force[t * rows + g * half + h + 1, s] += added[
                            g * kp : (g + 1) * kp, h * LANES : (h + 1) * LANES
                        ]

        def first(t, r, at):
            for s in range(subs):
                ya[at, s] = row(coef, t * subs + s, r) * force[at, s]

        sweep(first)

        def adjoint(src, dst):
            def body(t, r, at):
                sums = neighbour_sum(src, at)
                for s in range(subs):
                    dst[at, s] = row(coef, t * subs + s, r) * (force[at, s] + sums[s])

            sweep(body)

        src = ya
        for turn in range(SWEEPS - 2):
            dst = yb if src is ya else ya
            adjoint(src, dst)
            src = dst
        scaled = src

        @pl.loop(0, tiles)
        def _(t):
            totals = [jnp.zeros((2 * per, LANES), F32) for s in range(subs)]
            for r0 in range(0, rows, step):
                grads = [[] for s in range(subs)]
                for r in range(r0, r0 + step):
                    at = t * rows + r + 1
                    sums = neighbour_sum(scaled, at)
                    for s in range(subs):
                        b = t * subs + s
                        whole = (force[at, s] + sums[s]) * row(coef, b, rows + r)
                        grads[s].append(
                            -(
                                row(field, b, r) * whole[:per]
                                + row(field, b, rows + r) * whole[per:]
                            )
                        )
                for s in range(subs):
                    grad = jnp.concatenate(grads[s], axis=1)
                    top = grad.astype(BF)
                    low = (grad - top.astype(F32)).astype(BF)
                    hot = one_hot(wide(field, t * subs + s, cell_at + r0, count=step), LANES)
                    totals[s] += lax.dot_general(
                        jnp.concatenate([top, low], axis=0), hot, LAST, preferred_element_type=F32
                    )
            for s in range(subs):
                b = t * subs + s
                out[b, pl.ds(pl.multiple_of(chunk * per, 8), per), :] = (
                    totals[s][:per] + totals[s][per:]
                ) * (row(left, b, probes) + row(left, b, probes + 1) + row(left, b, probes + 2))

    if chunks == 1:
        one_chunk(0)
    else:
        finish_fetches()
        pl.loop(0, chunks)(one_chunk)


def owner_part(counts, field, drawn, pix, weight, prec, subs, rows, probes):
    blocks, slots, pixels = weight.shape
    grid_rows = blocks // subs * rows
    per = probes
    while per > 8 and grid_rows * subs * 2 * per * LANES * 4 > 9 * 2**20:
        per //= 2
    grid = pltpu.VMEM((grid_rows + 2, subs, 2 * per, LANES), F32)
    vmem = pl.BlockSpec(memory_space=pltpu.VMEM)
    return pl.pallas_call(
        functools.partial(owner_kernel, (subs, rows, per, probes // per, slots)),
        out_shape=jax.ShapeDtypeStruct((blocks, probes, LANES), F32),
        in_specs=[pl.BlockSpec(memory_space=pltpu.SMEM)] + [vmem] * 3 + [pl.BlockSpec(memory_space=pl.ANY)] * 2,
        out_specs=vmem,
        scratch_shapes=[
            grid,
            grid,
            grid,
            pltpu.VMEM((blocks * slots * (per + PAD), LANES), F32),
            pltpu.VMEM((rows * LANES // 256 * 2 * per, 256), BF),
            pltpu.VMEM((blocks, 2 * rows, LANES), F32),
            pltpu.VMEM(pix.shape, F32),
            pltpu.VMEM(drawn.shape, F32),
            pltpu.VMEM(prec.shape, BF),
            pltpu.VMEM(prec.shape, BF),
            pltpu.VMEM(weight.shape, F32),
            pltpu.VMEM(prec.shape, F32),
            pltpu.SemaphoreType.DMA((2,)),
        ],
        compiler_params=pltpu.CompilerParams(vmem_limit_bytes=56 * 2**20),
    )(counts, field, drawn, pix, weight, prec)


MESH = pl.DeviceIdType.MESH


def place():
    subs = lax.axis_size("sub")
    count = lax.axis_size("tile") * subs
    me = lax.axis_index("tile") * subs + lax.axis_index("sub")
    core = lax.axis_index("probe")

    def device(index):
        return {"tile": index // subs, "sub": index % subs}

    return count, me, core, device, {"probe": 1 - core}


def greet(count, me, device, partner):
    barrier = pltpu.get_barrier_semaphore()

    @pl.loop(1, count)
    def _(step):
        pl.semaphore_signal(
            barrier, inc=1, device_id=device((me + step) % count), device_id_type=MESH
        )

    pl.semaphore_signal(barrier, inc=1, device_id=partner, device_id_type=MESH)
    pl.semaphore_wait(barrier, count)


def entry_kernel(mesh_in, drawn_in, pix_in, mesh, drawn, pix, sent, came, passed, got):
    count, me, core, device, partner = place()
    greet(count, me, device, partner)

    def direct(source, peer, at):
        def copy(src, dst, k):
            return pltpu.make_async_remote_copy(
                src_ref=src,
                dst_ref=dst,
                send_sem=sent.at[k, source],
                recv_sem=came.at[k, at],
                device_id=device(peer),
                device_id_type=MESH,
            )

        return (
            copy(mesh_in.at[core], mesh.at[at, core], 0),
            copy(pix_in.at[peer, core], pix.at[at, core], 1),
            copy(drawn_in, drawn.at[at], 2),
        )

    def onward(source):
        def copy(ref, k):
            return pltpu.make_async_remote_copy(
                src_ref=ref.at[source, core],
                dst_ref=ref.at[source, core],
                send_sem=passed.at[k, source],
                recv_sem=got.at[k, source],
                device_id=partner,
                device_id_type=MESH,
            )

        return copy(mesh, 0), copy(pix, 1)

    def landed(source):
        def copy(ref, k):
            return pltpu.make_async_remote_copy(
                src_ref=ref.at[source, 1 - core],
                dst_ref=ref.at[source, 1 - core],
                send_sem=passed.at[k, source],
                recv_sem=got.at[k, source],
                device_id=partner,
                device_id_type=MESH,
            )

        return copy(mesh, 0), copy(pix, 1)

    @pl.loop(1, count)
    def _(step):
        peer = (me + step) % count
        for copy in direct(peer, peer, me):
            copy.start()

    mesh[me] = mesh_in[...]
    drawn[me] = drawn_in[...]
    pix[me] = pix_in[me]

    @pl.loop(1, count)
    def _(step):
        source = (me + count - step) % count
        first, second, third = direct(source, source, source)
        first.wait_recv()
        onward(source)[0].start()
        second.wait_recv()
        onward(source)[1].start()
        third.wait_recv()

    @pl.loop(1, count)
    def _(step):
        source = (me + count - step) % count
        for copy in landed(source):
            copy.wait_recv()
        for copy in onward(source):
            copy.wait_send()
        for copy in direct(source, source, me):
            copy.wait_send()


def entry(mesh_part, drawn, pix, count):
    vmem = pl.BlockSpec(memory_space=pltpu.VMEM)
    return pl.pallas_call(
        entry_kernel,
        out_shape=(
            jax.ShapeDtypeStruct((count,) + mesh_part.shape, mesh_part.dtype),
            jax.ShapeDtypeStruct((count,) + drawn.shape, drawn.dtype),
            jax.ShapeDtypeStruct(pix.shape, pix.dtype),
        ),
        in_specs=[vmem] * 3,
        out_specs=(vmem,) * 3,
        scratch_shapes=[
            pltpu.SemaphoreType.DMA((3, count)),
            pltpu.SemaphoreType.DMA((3, count)),
            pltpu.SemaphoreType.DMA((2, count)),
            pltpu.SemaphoreType.DMA((2, count)),
        ],
        compiler_params=pltpu.CompilerParams(
            collective_id=0, has_side_effects=True, vmem_limit_bytes=40 * 2**20
        ),
    )(mesh_part, drawn, pix)


def exit_kernel(part, signs, hess, diag, held, own, other, sent, came, side):
    count, me, core, device, partner = place()
    greet(count, me, device, partner)

    def copy(peer, at):
        return pltpu.make_async_remote_copy(
            src_ref=part.at[peer],
            dst_ref=held.at[at],
            send_sem=sent.at[peer],
            recv_sem=came.at[at],
            device_id=device(peer),
            device_id_type=MESH,
        )

    @pl.loop(1, count)
    def _(step):
        copy((me + step) % count, me).start()

    def add(step, total):
        source = (me + count - step) % count
        copy(source, source).wait_recv()
        return total + held[source]

    total = lax.fori_loop(1, count, add, part[me])
    hess[...] = total
    own[...] = jnp.broadcast_to(jnp.sum(signs[...] * total, axis=0, keepdims=True), own.shape)
    swap = pltpu.make_async_remote_copy(
        src_ref=own,
        dst_ref=other,
        send_sem=side.at[0],
        recv_sem=side.at[1],
        device_id=partner,
        device_id_type=MESH,
    )
    swap.start()

    @pl.loop(1, count)
    def _(step):
        copy((me + step) % count, me).wait_send()

    swap.wait()
    diag[...] = (own[...] + other[...]) * (1.0 / (2 * signs.shape[0]))


def exit_part(part, signs):
    count, probes, cells = part.shape
    vmem = pl.BlockSpec(memory_space=pltpu.VMEM)
    return pl.pallas_call(
        exit_kernel,
        out_shape=(
            jax.ShapeDtypeStruct((probes, cells), F32),
            jax.ShapeDtypeStruct((8, cells), F32),
        ),
        in_specs=[vmem] * 2,
        out_specs=(vmem,) * 2,
        scratch_shapes=[
            pltpu.VMEM(part.shape, F32),
            pltpu.VMEM((8, cells), F32),
            pltpu.VMEM((8, cells), F32),
            pltpu.SemaphoreType.DMA((count,)),
            pltpu.SemaphoreType.DMA((count,)),
            pltpu.SemaphoreType.DMA((2,)),
        ],
        compiler_params=pltpu.CompilerParams(
            collective_id=1, has_side_effects=True, vmem_limit_bytes=40 * 2**20
        ),
    )(part, signs)


def shards(
    base_velocity,
    viscosity,
    friction,
    cell_map,
    probe_signs,
    param_scale,
    track_nodes,
    los_coeff,
    pixel_weight,
    track_precision,
    slot_count,
):
    rows, cols = viscosity.shape
    cells = param_scale.shape[0]
    probes = probe_signs.shape[0]
    subs = lax.axis_size("sub")
    count = lax.axis_size("tile") * subs
    myself = lax.axis_index("tile") * subs + lax.axis_index("sub")
    signed = (2 * probe_signs - 1).astype(F32)
    mesh_part = jnp.concatenate(
        [
            base_velocity.reshape(2 * rows, cols),
            viscosity,
            friction,
            (cell_map - myself * cells).astype(F32),
        ],
        axis=0,
    ).reshape(2, 5 * rows // 2, cols)
    top = lax.reduce_precision(param_scale, 8, 7)
    mid = lax.reduce_precision(param_scale - top, 8, 7)
    low = param_scale - top - mid
    drawn = jnp.concatenate(
        [signed, top[None], mid[None], low[None], jnp.zeros((13, cells), F32)], axis=0
    ).astype(BF)
    nodes = track_nodes[0]
    slots = nodes.shape[1]
    planes = jnp.concatenate(
        [
            (nodes // 256).astype(BF),
            (nodes % 256).astype(BF),
            los_coeff[0, 0].astype(BF),
            los_coeff[1, 0].astype(BF),
        ],
        axis=1,
    ).reshape(count, 2, 2 * slots, LANES)
    field, drawn, pix = entry(mesh_part, drawn, planes, count)
    counts = jnp.take(slot_count, myself, axis=1)
    part = owner_part(
        counts,
        field.reshape(count, 5 * rows, cols),
        drawn,
        pix.reshape(count, 4 * slots, LANES),
        pixel_weight[:, 0],
        track_precision[0],
        subs,
        rows,
        probes,
    )
    hess_probe, diag = exit_part(part, signed)
    return (hess_probe, diag[0])


def solution(mesh):
    placed = (
        P(None, "tile", "sub"),
        P("tile", "sub"),
        P("tile", "sub"),
        P("tile", "sub"),
        P("probe", ("tile", "sub")),
        P(("tile", "sub")),
        P(("tile", "sub"), None, None, None),
        P(None, ("tile", "sub"), None, None, None),
        P(None, ("tile", "sub"), None, None),
        P(("tile", "sub"), None, None),
        P(),
    )
    return jax.shard_map(
        shards,
        mesh=mesh,
        in_specs=placed,
        out_specs=(P("probe", ("tile", "sub")), P(("tile", "sub"))),
        check_vma=False,
    )
```
